1024 devices in a mesh: ctx: 128 (over x, y, z_hi), head: 8 (over z_lo, core).
Axes of the slice: x: 8, y: 8, z: 8 (z_hi: 2, z_lo: 4; z = z_hi * 4 + z_lo), core: 2. Of those that a mesh axis runs over, the one named last changes fastest.
Arguments:
- query_nope: bfloat16 [16384, 8192], P('ctx', 'head'), may hold values from -6 to 6
- query_rope: bfloat16 [16384, 4096], P('ctx', 'head'), may hold values from -450 to 450
- grad_out: bfloat16 [16384, 8192], P('ctx', 'head'), may hold values from -24 to 24
- latent: bfloat16 [16384, 576], P(('ctx', 'head')), may hold values from -8 to 8
- key_up: bfloat16 [512, 8192], P(None, 'head'), may hold values from -0.25 to 0.25
- value_up: bfloat16 [512, 8192], P(None, 'head'), may hold values from -0.25 to 0.25
- block_keep: int32 [128, 3], P('ctx'), may hold values 0 or 1
Outputs:
- d_query_nope: float32 [16384, 8192], P('ctx', 'head')
- d_query_rope: float32 [16384, 4096], P('ctx', 'head')
- d_latent: float32 [16384, 576], P(('ctx', 'head'))
The draws below stay inside these ranges and needn't reach their ends.
All inputs are finite; a program needn't handle non-finite values. No bound on the sum of `block_keep` on one device may be relied on, other than what follows from the above.
Results may differ from the reference program's by a relative error of at most 0.015.
Values may be sent and summed in bfloat16 or wider, within the bound.
No kernel may reach another device: no remote copies, remote signals or barrier semaphores. Data moves between devices by JAX's collectives and lax.ppermute only.
A program may use at most 32 MiB of HBM per device.

```python
import math
import jax
import jax.numpy as jnp
from jax import lax

HEADS = 64
NOPE = 128
ROPE = 64
VDIM = 128
RANK = 512
STEPS = 3
GROUP = 128
LATENT = 576
TOKENS = 16384
NBLOCKS = 128
N_CTX = 128


def draw_latent(key, part):
    drawn = jnp.clip(jax.random.normal(jax.random.fold_in(key, 1), (TOKENS, LATENT), jnp.float32), -6.0, 6.0)
    return drawn.astype(jnp.bfloat16)


def draw_query_rope(key, part):
    drawn = jnp.clip(jax.random.normal(jax.random.fold_in(key, 3), (TOKENS, HEADS * ROPE), jnp.float32), -6.0, 6.0)
    return drawn.astype(jnp.bfloat16)


def draw_query_nope(key, part):
    drawn = jnp.clip(jax.random.normal(jax.random.fold_in(key, 5), (TOKENS, HEADS * NOPE), jnp.float32), -6.0, 6.0)
    return drawn.astype(jnp.bfloat16)


def set_ends(values, own_key, low, high):
    longest = values.shape.index(max(values.shape))
    spots = []
    for shift in (0, 1):
        where = [jax.random.randint(jax.random.fold_in(own_key, axis), (), 0, length) for axis, length in enumerate(values.shape)]
        where[longest] = (where[longest] + shift) % values.shape[longest]
        spots.append(tuple(where))
    return values.at[spots[0]].set(low).at[spots[1]].set(high)


def levels(own_key, dims, split, low, high):
    loudness, own = 1.0, jax.random.fold_in(own_key, 6)
    for dim, shards_of in split:
        heights = jnp.exp(jax.random.uniform(jax.random.fold_in(own, dim), (shards_of,), jnp.float32, low / len(split), high / len(split)))
        loudness = loudness * jnp.repeat(heights, dims[dim] // shards_of).reshape([-1 if axis == dim else 1 for axis in range(len(dims))])
    return loudness


def scatter_about(stream_key, dims, width, limit, split=(), held_as=jnp.bfloat16):
    factor_of = levels(stream_key, dims, split, -0.22, 0.18) if split else 1.0
    array = jax.random.normal(stream_key, dims, jnp.float32) * width * factor_of
    return jnp.minimum(jnp.maximum(array, -limit), limit).astype(held_as)


def setup_inputs(seed: int = 0) -> dict:
    seeds = jax.random.split(jax.random.key(seed), 8)
    query_nope = draw_query_nope(jax.random.fold_in(seeds[7], 71), 0)
    query_rope = draw_query_rope(jax.random.fold_in(seeds[7], 71), 0)
    grad_out = scatter_about(seeds[2], (TOKENS, HEADS * VDIM), 4.0, 24.0, ((0, 128), (1, 8)))
    latent = draw_latent(jax.random.fold_in(seeds[7], 71), 0)
    key_up = scatter_about(seeds[4], (RANK, HEADS * NOPE), RANK ** -0.5, 0.25, ((1, 8),))
    value_up = scatter_about(seeds[5], (RANK, HEADS * VDIM), RANK ** -0.5, 0.25, ((1, 8),))
    block_keep = set_ends((jax.random.randint(seeds[6], (NBLOCKS, STEPS), 0, 4) < 3).astype(jnp.int32), jax.random.fold_in(seeds[6], 1), 0, 1)
    return {"query_nope": query_nope, "query_rope": query_rope, "grad_out": grad_out, "latent": latent, "key_up": key_up, "value_up": value_up, "block_keep": block_keep}


def window_mask(group_len, cycle_steps, keep_row, position):
    grid_shape = (group_len, cycle_steps + 1, group_len)
    query_at = lax.broadcasted_iota(jnp.int32, grid_shape, 0)
    block_at = lax.broadcasted_iota(jnp.int32, grid_shape, 1)
    key_at = lax.broadcasted_iota(jnp.int32, grid_shape, 2)
    blocks_back = cycle_steps - block_at
    block_flags = jnp.concatenate([keep_row[::-1], jnp.ones((1,), jnp.int32)])
    kept_block = block_flags[None, :, None] == 1
    in_range = position - blocks_back >= 0
    causal = (blocks_back > 0) | (key_at <= query_at)
    return (kept_block & in_range & causal).reshape(group_len, (cycle_steps + 1) * group_len)

def block_grads(query_nope, query_rope, grad_out, keys_nope, values, keys_rope, key_up, value_up, allowed):
    group_len = query_nope.shape[0]
    window_len = keys_nope.shape[0]
    head_count = key_up.shape[1] // NOPE
    score_scale = 1.0 / math.sqrt(NOPE + ROPE)
    query_heads = query_nope.reshape(group_len, head_count, NOPE).astype(jnp.float32)
    rope_heads = query_rope.reshape(group_len, head_count, ROPE).astype(jnp.float32)
    out_heads = grad_out.reshape(group_len, head_count, VDIM).astype(jnp.float32)
    key_heads = keys_nope.reshape(window_len, head_count, NOPE).astype(jnp.float32)
    value_heads = values.reshape(window_len, head_count, VDIM).astype(jnp.float32)
    rope_keys = keys_rope.astype(jnp.float32)
    scores = (jnp.einsum('chd,khd->hck', query_heads, key_heads) + jnp.einsum('chd,kd->hck', rope_heads, rope_keys)) * score_scale
    scores = jnp.where(allowed[None], scores, -jnp.inf)
    row_top = lax.optimization_barrier(jnp.max(scores, axis=2, keepdims=True))
    exponent = jnp.exp(scores - row_top)
    probs = exponent / lax.optimization_barrier(jnp.sum(exponent, axis=2, keepdims=True))
    weights = probs.astype(jnp.bfloat16)
    output = jnp.einsum('hck,khd->chd', weights.astype(jnp.float32), value_heads)
    row_delta = lax.optimization_barrier(jnp.sum(output * out_heads, axis=2))
    slopes = jnp.einsum('chd,khd->hck', out_heads, value_heads)
    score_grad = (probs * (slopes - row_delta.T[:, :, None]) * score_scale).astype(jnp.bfloat16)
    grad_f32 = score_grad.astype(jnp.float32)
    query_grad_nope = jnp.einsum('hck,khd->chd', grad_f32, key_heads).reshape(group_len, head_count * NOPE)
    query_grad_rope = jnp.einsum('hck,kd->chd', grad_f32, rope_keys).reshape(group_len, head_count * ROPE)
    key_grad = jnp.einsum('hck,chd->khd', grad_f32, query_heads).astype(jnp.bfloat16).reshape(window_len, head_count * NOPE)
    rope_grad = jnp.einsum('hck,chd->kd', grad_f32, rope_heads)
    value_grad = jnp.einsum('hck,chd->khd', weights.astype(jnp.float32), out_heads).astype(jnp.bfloat16).reshape(window_len, head_count * VDIM)
    content_grad = jnp.dot(key_grad, key_up.T, preferred_element_type=jnp.float32) + jnp.dot(value_grad, value_up.T, preferred_element_type=jnp.float32)
    return (query_grad_nope, query_grad_rope, jnp.concatenate([content_grad, rope_grad], axis=1))

def reference(query_nope, query_rope, grad_out, latent, key_up, value_up, block_keep):
    content = latent[:, :RANK]
    keys_nope = jnp.dot(content, key_up, preferred_element_type=jnp.float32).astype(jnp.bfloat16)
    values = jnp.dot(content, value_up, preferred_element_type=jnp.float32).astype(jnp.bfloat16)
    keys_rope = latent[:, RANK:]
    lead_rows = STEPS * GROUP
    window_len = (STEPS + 1) * GROUP

    def pad_front(source_rows):
        return jnp.concatenate([jnp.zeros((lead_rows, source_rows.shape[1]), source_rows.dtype), source_rows], axis=0)
    padded_nope = pad_front(keys_nope)
    padded_values = pad_front(values)
    padded_rope = pad_front(keys_rope)

    def one_block(carried, block_index):
        row_start = (block_index * GROUP).astype(jnp.int32)
        query_rows = lax.dynamic_slice_in_dim(query_nope, row_start, GROUP, 0)
        rope_rows = lax.dynamic_slice_in_dim(query_rope, row_start, GROUP, 0)
        out_rows = lax.dynamic_slice_in_dim(grad_out, row_start, GROUP, 0)
        window_nope = lax.dynamic_slice_in_dim(padded_nope, row_start, window_len, 0)
        window_values = lax.dynamic_slice_in_dim(padded_values, row_start, window_len, 0)
        window_rope = lax.dynamic_slice_in_dim(padded_rope, row_start, window_len, 0)
        keep_row = lax.dynamic_index_in_dim(block_keep, block_index, 0, keepdims=False)
        allowed = window_mask(GROUP, STEPS, keep_row, block_index)
        grad_nope, grad_rope, partial_value = block_grads(query_rows, rope_rows, out_rows, window_nope, window_values, window_rope, key_up, value_up, allowed)
        current = lax.dynamic_slice_in_dim(carried, row_start, window_len, 0)
        carried = lax.dynamic_update_slice_in_dim(carried, current + partial_value, row_start, 0)
        return (carried, (grad_nope, grad_rope))
    carried, (grads_nope, grads_rope) = lax.scan(one_block, jnp.zeros((lead_rows + TOKENS, LATENT), jnp.float32), jnp.arange(N_CTX, dtype=jnp.int32))
    return (grads_nope.reshape(TOKENS, HEADS * NOPE), grads_rope.reshape(TOKENS, HEADS * ROPE), carried[lead_rows:])
```

```python
import math

import jax
import jax.numpy as jnp
import numpy as np
from jax import lax
from jax.experimental import pallas as pl
from jax.experimental.pallas import tpu as pltpu
from jax.sharding import Mesh, PartitionSpec as P

NOPE = 128
ROPE = 64
VDIM = 128
RANK = 512
WIDTH = RANK + ROPE
SCALE = 1.0 / math.sqrt(NOPE + ROPE)
LOG2E = 1.4426950408889634
BF16 = jnp.bfloat16
F32 = jnp.float32
NT = (((1,), (1,)), ((), ()))
TN = (((0,), (0,)), ((), ()))
VMEM = pl.BlockSpec(memory_space=pltpu.VMEM)
SMEM = pl.BlockSpec(memory_space=pltpu.SMEM)
PARAMS = pltpu.CompilerParams(vmem_limit_bytes=48 * 1024 * 1024)


def dot(a, b, dims=(((1,), (0,)), ((), ()))):
    return lax.dot_general(a, b, dims, preferred_element_type=F32)


def absorb_kernel(where_ref, keep_ref, qn_ref, qr_ref, go_ref, kup_ref, vup_ref, ql_ref, g_ref, bias_ref):
    heads = kup_ref.shape[1] // NOPE
    group = qn_ref.shape[0]
    for h in range(heads):
        rows = pl.ds(h * group, group)
        cols = pl.ds(h * NOPE, NOPE)
        ql_ref[rows, :RANK] = dot(qn_ref[:, cols], kup_ref[:, cols], NT).astype(BF16)
        ql_ref[rows, RANK:] = qr_ref[:, pl.ds(h * ROPE, ROPE)]
        g_ref[rows, :] = dot(go_ref[:, cols], vup_ref[:, cols], NT).astype(BF16)
    col, hi, core = where_ref[0], where_ref[1], where_ref[2]
    position = 2 * col + hi
    row = lax.broadcasted_iota(jnp.int32, bias_ref.shape, 0)
    query = lax.broadcasted_iota(jnp.int32, bias_ref.shape, 1)
    low = row & 15
    slot = (row >> 4) & 1
    lo = (row >> 5) & 3
    source = (row >> 7) & 1
    side = (row >> 8) ^ core
    back_even = jnp.where(slot == 0, 3 * source, 2 - source)
    back_odd = jnp.where(slot == 0, 1 - source, 3 - source)
    back = jnp.where(hi == 0, back_even, back_odd)
    token = (lo * 2 + side) * 16 + low
    kept = jnp.where(
        back == 1, keep_ref[0, 0], jnp.where(back == 2, keep_ref[0, 1], keep_ref[0, 2])
    )
    seen = jnp.where(
        back == 0,
        (token <= query).astype(jnp.int32),
        ((kept == 1) & (position >= back)).astype(jnp.int32),
    )
    bias_ref[...] = jnp.where(seen == 1, 0.0, -jnp.inf)


def attend_kernel(mine_ref, mate_ref, ql_ref, g_ref, bias_ref, send_ref, ds_ref, wt_ref, lat_ref):
    half = mine_ref.shape[0]
    group = bias_ref.shape[1]
    pairs = ql_ref.shape[0] // (2 * group)
    lat_ref[:half] = mine_ref[...]
    lat_ref[half:] = mate_ref[...]
    for pair in range(pairs):
        cols = pl.ds(pair * 2 * group, 2 * group)
        bias = bias_ref[...]
        bias = jnp.concatenate([bias, bias], axis=1)
        scores = dot(lat_ref[...], ql_ref[cols, :], NT) * (SCALE * LOG2E) + bias
        top = jnp.max(scores, axis=0, keepdims=True)
        exponent = jnp.exp2(scores - top)
        probs = exponent * (1.0 / jnp.sum(exponent, axis=0, keepdims=True))
        weights = probs.astype(BF16)
        wt_ref[:, cols] = weights
        slopes = dot(lat_ref[:, :RANK], g_ref[cols, :], NT)
        delta = jnp.sum(weights.astype(F32) * slopes, axis=0, keepdims=True)
        ds_ref[:, cols] = (probs * ((slopes - delta) * SCALE)).astype(BF16)
    content = dot(ds_ref[half:, :], ql_ref[:, :RANK]) + dot(wt_ref[half:, :], g_ref[...])
    send_ref[:, :RANK] = content.astype(BF16)
    send_ref[:, RANK:] = dot(ds_ref[half:, :], ql_ref[:, RANK:]).astype(BF16)


def own_kernel(ds_ref, wt_ref, ql_ref, g_ref, own_ref):
    half = own_ref.shape[0]
    content = dot(ds_ref[:half, :], ql_ref[:, :RANK]) + dot(wt_ref[:half, :], g_ref[...])
    own_ref[:, :RANK] = content
    own_ref[:, RANK:] = dot(ds_ref[:half, :], ql_ref[:, RANK:])


def query_kernel(mine_ref, mate_ref, ds_ref, kup_ref, dqn_ref, dqr_ref):
    half = mine_ref.shape[0]
    group = dqn_ref.shape[0]
    heads = kup_ref.shape[1] // NOPE
    for h in range(heads):
        cols = pl.ds(h * group, group)
        absorbed = dot(ds_ref[:half, cols], mine_ref[...], TN) + dot(ds_ref[half:, cols], mate_ref[...], TN)
        nope = pl.ds(h * NOPE, NOPE)
        dqn_ref[:, nope] = dot(absorbed[:, :RANK].astype(BF16), kup_ref[:, nope])
        dqr_ref[:, pl.ds(h * ROPE, ROPE)] = absorbed[:, RANK:]


def call(kernel, outs, specs, scratch=(), flops=0, nbytes=0):
    return pl.pallas_call(
        kernel,
        out_shape=[jax.ShapeDtypeStruct(s, t) for s, t in outs],
        in_specs=specs,
        out_specs=[VMEM] * len(outs),
        scratch_shapes=scratch,
        compiler_params=PARAMS,
        cost_estimate=pl.CostEstimate(flops=flops, bytes_accessed=nbytes, transcendentals=0),
    )


def on_device(query_nope, query_rope, grad_out, latent, key_up, value_up, block_keep):
    group = query_nope.shape[0]
    rows, width = latent.shape
    heads = key_up.shape[1] // NOPE
    columns = lax.axis_size("col")
    chips = lax.axis_size("hi") * lax.axis_size("lo")
    chips_lo = lax.axis_size("lo")
    total = heads * group
    window = 4 * group
    half = window // 2
    hi = lax.axis_index("hi")
    where = jnp.stack([lax.axis_index("col"), hi, lax.axis_index("core")]).astype(jnp.int32)

    back1 = lax.ppermute(latent, "col", [(i, i + 1) for i in range(columns - 1)])
    back2 = lax.ppermute(latent, ("col", "hi"), [(2 * i + 1, 2 * i + 5) for i in range(columns - 2)])

    ql, g, bias = call(
        absorb_kernel,
        [((total, width), BF16), ((total, RANK), BF16), ((window, group), F32)],
        [SMEM, SMEM] + [VMEM] * 5,
        flops=4 * total * NOPE * RANK,
        nbytes=5 << 20,
    )(where, block_keep, query_nope, query_rope, grad_out, key_up, value_up)

    to_even = jnp.concatenate([jnp.where(hi == 1, back2, latent), back1], axis=0)
    to_odd = jnp.concatenate([latent, back1], axis=0)
    pieces = jnp.concatenate(
        [jnp.broadcast_to(p, (chips_lo, 2 * rows, width)) for p in (to_even, to_odd)], axis=0
    )
    mine = lax.all_to_all(pieces, ("hi", "lo"), 0, 0, tiled=True).reshape(half, width)
    swap = [(0, 1), (1, 0)]
    mate = lax.ppermute(mine, "core", swap)

    send, ds, wt = call(
        attend_kernel,
        [((half, width), BF16), ((window, total), BF16), ((window, total), BF16)],
        [VMEM] * 5,
        scratch=[pltpu.VMEM((window, width), BF16)],
        flops=6 * total * window * width,
        nbytes=5 << 20,
    )(mine, mate, ql, g, bias)
    arrived = lax.ppermute(send, "core", swap)
    (own,) = call(
        own_kernel,
        [((half, width), F32)],
        [VMEM] * 4,
        flops=4 * half * total * width,
        nbytes=4 << 20,
    )(ds, wt, ql, g)
    summed = (own + arrived.astype(F32)).astype(BF16).reshape(chips, 2 * rows, width)
    parts = lax.all_to_all(summed, ("hi", "lo"), 0, 0, tiled=True)
    d_nope, d_rope = call(
        query_kernel,
        [((group, heads * NOPE), F32), ((group, heads * ROPE), F32)],
        [VMEM] * 4,
        flops=2 * total * window * width + 2 * total * RANK * NOPE,
        nbytes=4 << 20,
    )(mine, mate, ds, key_up)
    parts = parts.reshape(2, chips_lo, 2, rows, width).astype(F32)
    sums = jnp.sum(parts, axis=1)
    from_even = sums[0, 0]
    local = sums[1, 0] + jnp.where(hi == 0, from_even, 0.0)
    to_back1 = (sums[0, 1] + sums[1, 1]).astype(BF16)
    to_back2 = from_even.astype(BF16)
    came1 = lax.ppermute(to_back1, "col", [(i + 1, i) for i in range(columns - 1)])
    came2 = lax.ppermute(to_back2, ("col", "hi"), [(2 * i + 5, 2 * i + 1) for i in range(columns - 2)])
    d_latent = local + came1.astype(F32) + came2.astype(F32)
    return (d_nope, d_rope, d_latent)


def solution(mesh):
    fine = Mesh(mesh.devices.reshape(-1, 2, 4, 2), ("col", "hi", "lo", "core"))
    ctx, head = ("col", "hi"), ("lo", "core")
    placed = (
        P(ctx, head),
        P(ctx, head),
        P(ctx, head),
        P((*ctx, *head), None),
        P(None, head),
        P(None, head),
        P(ctx, None),
    )
    return jax.shard_map(
        on_device,
        mesh=fine,
        in_specs=placed,
        out_specs=(P(ctx, head), P(ctx, head), P((*ctx, *head), None)),
        check_vma=False,
    )
```

```python
import math

import jax
import jax.numpy as jnp
import numpy as np
from jax import lax
from jax.experimental import pallas as pl
from jax.experimental.pallas import tpu as pltpu
from jax.sharding import Mesh, PartitionSpec as P

NOPE = 128
ROPE = 64
VDIM = 128
RANK = 512
WIDTH = RANK + ROPE
SCALE = 1.0 / math.sqrt(NOPE + ROPE)
LOG2E = 1.4426950408889634
EARLY = 2
BF16 = jnp.bfloat16
F32 = jnp.float32
NT = (((1,), (1,)), ((), ()))
TN = (((0,), (0,)), ((), ()))
VMEM = pl.BlockSpec(memory_space=pltpu.VMEM)
SMEM = pl.BlockSpec(memory_space=pltpu.SMEM)
PARAMS = pltpu.CompilerParams(vmem_limit_bytes=16 * 1024 * 1024)


def dot(a, b, dims=(((1,), (0,)), ((), ()))):
    return lax.dot_general(a, b, dims, preferred_element_type=F32)


def absorb_kernel(where_ref, keep_ref, qn_ref, qr_ref, go_ref, kup_ref, vup_ref, ql_ref, g_ref, bias_ref):
    heads = kup_ref.shape[1] // NOPE
    group = qn_ref.shape[0]
    for h in range(heads):
        rows = pl.ds(h * group, group)
        cols = pl.ds(h * NOPE, NOPE)
        ql_ref[rows, :RANK] = dot(qn_ref[:, cols], kup_ref[:, cols], NT).astype(BF16)
        ql_ref[rows, RANK:] = qr_ref[:, pl.ds(h * ROPE, ROPE)]
        g_ref[rows, :] = dot(go_ref[:, cols], vup_ref[:, cols], NT).astype(BF16)
    col, hi, core = where_ref[0], where_ref[1], where_ref[2]
    position = 2 * col + hi
    row = lax.broadcasted_iota(jnp.int32, bias_ref.shape, 0)
    query = lax.broadcasted_iota(jnp.int32, bias_ref.shape, 1)
    low = row & 15
    slot = (row >> 4) & 1
    lo = (row >> 5) & 3
    source = (row >> 7) & 1
    side = (row >> 8) ^ core
    back_even = jnp.where(slot == 0, 3 * source, 2 - source)
    back_odd = jnp.where(slot == 0, 1 - source, 3 - source)
    back = jnp.where(hi == 0, back_even, back_odd)
    token = (lo * 2 + side) * 16 + low
    kept = jnp.where(
        back == 1, keep_ref[0, 0], jnp.where(back == 2, keep_ref[0, 1], keep_ref[0, 2])
    )
    seen = jnp.where(
        back == 0,
        (token <= query).astype(jnp.int32),
        ((kept == 1) & (position >= back)).astype(jnp.int32),
    )
    bias_ref[...] = jnp.where(seen == 1, 0.0, -jnp.inf)


def stage_kernel(in_ref, out_ref):
    out_ref[...] = in_ref[...]


def pieces_kernel(latent_ref, back1_ref, back2_ref, out_ref):
    rows = latent_ref.shape[0]
    chips_lo = out_ref.shape[0] // 2
    own, back1 = latent_ref[...], back1_ref[...]
    to_even = jnp.where(lax.axis_index("hi") == 1, back2_ref[...], own)
    for i in range(2 * chips_lo):
        out_ref[i, :rows] = to_even if i < chips_lo else own
        out_ref[i, rows:] = back1


def attend_kernel(mine_ref, mate_ref, ql_ref, g_ref, bias_ref, send_ref, ds_ref, wt_ref, lat_ref):
    half = mine_ref.shape[0]
    group = bias_ref.shape[1]
    pairs = ql_ref.shape[0] // (2 * group)
    lat_ref[:half] = mine_ref[...]
    lat_ref[half:] = mate_ref[...]
    for pair in range(pairs):
        cols = pl.ds(pair * 2 * group, 2 * group)
        bias = bias_ref[...]
        bias = jnp.concatenate([bias, bias], axis=1)
        scores = dot(lat_ref[...], ql_ref[cols, :], NT) * (SCALE * LOG2E) + bias
        top = jnp.max(scores, axis=0, keepdims=True)
        exponent = jnp.exp2(scores - top)
        probs = exponent * (1.0 / jnp.sum(exponent, axis=0, keepdims=True))
        weights = probs.astype(BF16)
        wt_ref[:, cols] = weights
        slopes = dot(lat_ref[:, :RANK], g_ref[cols, :], NT)
        delta = jnp.sum(weights.astype(F32) * slopes, axis=0, keepdims=True)
        ds_ref[:, cols] = (probs * ((slopes - delta) * SCALE)).astype(BF16)
    content = dot(ds_ref[half:, :], ql_ref[:, :RANK]) + dot(wt_ref[half:, :], g_ref[...])
    send_ref[:, :RANK] = content.astype(BF16)
    send_ref[:, RANK:] = dot(ds_ref[half:, :], ql_ref[:, RANK:]).astype(BF16)


def query_grads(heads, mine_ref, mate_ref, ds_ref, kup_ref, dqn_ref, dqr_ref):
    half = mine_ref.shape[0]
    group = dqn_ref.shape[0]
    for h in heads:
        cols = pl.ds(h * group, group)
        absorbed = dot(ds_ref[:half, cols], mine_ref[...], TN) + dot(ds_ref[half:, cols], mate_ref[...], TN)
        nope = pl.ds(h * NOPE, NOPE)
        dqn_ref[:, nope] = dot(absorbed[:, :RANK].astype(BF16), kup_ref[:, nope])
        dqr_ref[:, pl.ds(h * ROPE, ROPE)] = absorbed[:, RANK:]


def own_kernel(mine_ref, mate_ref, ds_ref, wt_ref, ql_ref, g_ref, kup_ref, own_ref, dqn_ref, dqr_ref):
    half = own_ref.shape[0]
    content = dot(ds_ref[:half, :], ql_ref[:, :RANK]) + dot(wt_ref[:half, :], g_ref[...])
    own_ref[:, :RANK] = content
    own_ref[:, RANK:] = dot(ds_ref[:half, :], ql_ref[:, RANK:])
    query_grads(range(EARLY), mine_ref, mate_ref, ds_ref, kup_ref, dqn_ref, dqr_ref)


def add_kernel(own_ref, arrived_ref, sum_ref):
    sum_ref[...] = (own_ref[...] + arrived_ref[...].astype(F32)).astype(BF16)


def query_kernel(mine_ref, mate_ref, ds_ref, kup_ref, early_n_ref, early_r_ref, dqn_ref, dqr_ref):
    dqn_ref[:, : EARLY * NOPE] = early_n_ref[...]
    dqr_ref[:, : EARLY * ROPE] = early_r_ref[...]
    heads = kup_ref.shape[1] // NOPE
    query_grads(range(EARLY, heads), mine_ref, mate_ref, ds_ref, kup_ref, dqn_ref, dqr_ref)


def owners_kernel(parts_ref, local_ref, to_back1_ref, to_back2_ref):
    chips_lo = parts_ref.shape[0] // 2
    rows = local_ref.shape[0]
    even = [parts_ref[i].astype(F32) for i in range(chips_lo)]
    odd = [parts_ref[chips_lo + i].astype(F32) for i in range(chips_lo)]
    even, odd = sum(even[1:], even[0]), sum(odd[1:], odd[0])
    to_back1_ref[...] = (even[rows:] + odd[rows:]).astype(BF16)
    to_back2_ref[...] = even[:rows].astype(BF16)
    local_ref[...] = odd[:rows] + jnp.where(lax.axis_index("hi") == 0, even[:rows], 0.0)


def call(kernel, outs, specs, scratch=(), flops=0, nbytes=0):
    return pl.pallas_call(
        kernel,
        out_shape=[jax.ShapeDtypeStruct(s, t) for s, t in outs],
        in_specs=specs,
        out_specs=[VMEM] * len(outs),
        scratch_shapes=scratch,
        compiler_params=PARAMS,
        cost_estimate=pl.CostEstimate(flops=flops, bytes_accessed=nbytes, transcendentals=0),
    )


def on_device(query_nope, query_rope, grad_out, latent, key_up, value_up, block_keep):
    group = query_nope.shape[0]
    rows, width = latent.shape
    heads = key_up.shape[1] // NOPE
    columns = lax.axis_size("col")
    chips = lax.axis_size("hi") * lax.axis_size("lo")
    total = heads * group
    window = 4 * group
    half = window // 2
    where = jnp.stack([lax.axis_index(name) for name in ("col", "hi", "core")]).astype(jnp.int32)

    back1 = lax.ppermute(latent, "col", [(i, i + 1) for i in range(columns - 1)])
    back2 = lax.ppermute(latent, ("col", "hi"), [(2 * i + 1, 2 * i + 5) for i in range(columns - 2)])

    ql, g, bias = call(
        absorb_kernel,
        [((total, width), BF16), ((total, RANK), BF16), ((window, group), F32)],
        [SMEM, SMEM] + [VMEM] * 5,
        flops=4 * total * NOPE * RANK,
        nbytes=5 << 20,
    )(where, block_keep, query_nope, query_rope, grad_out, key_up, value_up)
    (staged,) = call(stage_kernel, [((rows, width), BF16)], [VMEM], flops=4 << 30, nbytes=4 << 20)(latent)
    (pieces,) = call(
        pieces_kernel,
        [((chips, 2 * rows, width), BF16)],
        [VMEM] * 3,
        flops=4 << 30,
        nbytes=4 << 20,
    )(staged, back1, back2)
    mine = lax.all_to_all(pieces, ("hi", "lo"), 0, 0, tiled=True).reshape(half, width)
    swap = [(0, 1), (1, 0)]
    mate = lax.ppermute(mine, "core", swap)
    send, ds, wt = call(
        attend_kernel,
        [((half, width), BF16), ((window, total), BF16), ((window, total), BF16)],
        [VMEM] * 5,
        scratch=[pltpu.VMEM((window, width), BF16)],
        flops=6 * total * window * width,
        nbytes=5 << 20,
    )(mine, mate, ql, g, bias)
    arrived = lax.ppermute(send, "core", swap)
    own, early_n, early_r = call(
        own_kernel,
        [((half, width), F32), ((group, EARLY * NOPE), F32), ((group, EARLY * ROPE), F32)],
        [VMEM] * 7,
        flops=4 * half * total * width,
        nbytes=4 << 20,
    )(mine, mate, ds, wt, ql, g, key_up)
    (summed,) = call(add_kernel, [((half, width), BF16)], [VMEM] * 2)(own, arrived)
    parts = lax.all_to_all(summed.reshape(chips, 2 * rows, width), ("hi", "lo"), 0, 0, tiled=True)
    local, to_back1, to_back2 = call(
        owners_kernel,
        [((rows, width), F32), ((rows, width), BF16), ((rows, width), BF16)],
        [VMEM],
    )(parts)
    d_nope, d_rope = call(
        query_kernel,
        [((group, heads * NOPE), F32), ((group, heads * ROPE), F32)],
        [VMEM] * 6,
        flops=2 * total * window * width + 2 * total * RANK * NOPE,
        nbytes=4 << 20,
    )(mine, mate, ds, key_up, early_n, early_r)
    came2 = lax.ppermute(to_back2, ("col", "hi"), [(2 * i + 5, 2 * i + 1) for i in range(columns - 2)])
    came1 = lax.ppermute(to_back1, "col", [(i + 1, i) for i in range(columns - 1)])
    d_latent = local + came1.astype(F32) + came2.astype(F32)
    return (d_nope, d_rope, d_latent)


def solution(mesh):
    fine = Mesh(mesh.devices.reshape(-1, 2, 4, 2), ("col", "hi", "lo", "core"))
    ctx, head = ("col", "hi"), ("lo", "core")
    placed = (
        P(ctx, head),
        P(ctx, head),
        P(ctx, head),
        P((*ctx, *head), None),
        P(None, head),
        P(None, head),
        P(ctx, None),
    )
    return jax.shard_map(
        on_device,
        mesh=fine,
        in_specs=placed,
        out_specs=(P(ctx, head), P(ctx, head), P((*ctx, *head), None)),
        check_vma=False,
    )
```

```python
import math

import jax
import jax.numpy as jnp
import numpy as np
from jax import lax
from jax.experimental import pallas as pl
from jax.experimental.pallas import tpu as pltpu
from jax.sharding import Mesh, PartitionSpec as P

NOPE = 128
ROPE = 64
VDIM = 128
RANK = 512
WIDTH = RANK + ROPE
SCALE = 1.0 / math.sqrt(NOPE + ROPE)
LOG2E = 1.4426950408889634
EARLY = 2
BF16 = jnp.bfloat16
F32 = jnp.float32
NT = (((1,), (1,)), ((), ()))
TN = (((0,), (0,)), ((), ()))
VMEM = pl.BlockSpec(memory_space=pltpu.VMEM)
SMEM = pl.BlockSpec(memory_space=pltpu.SMEM)
PARAMS = pltpu.CompilerParams(vmem_limit_bytes=16 * 1024 * 1024)


def dot(a, b, dims=(((1,), (0,)), ((), ()))):
    return lax.dot_general(a, b, dims, preferred_element_type=F32)


def absorb_kernel(where_ref, keep_ref, qn_ref, qr_ref, go_ref, kup_ref, vup_ref, ql_ref, g_ref, bias_ref):
    heads = kup_ref.shape[1] // NOPE
    group = qn_ref.shape[0]
    for h in range(heads):
        rows = pl.ds(h * group, group)
        cols = pl.ds(h * NOPE, NOPE)
        ql_ref[rows, :RANK] = dot(qn_ref[:, cols], kup_ref[:, cols], NT).astype(BF16)
        ql_ref[rows, RANK:] = qr_ref[:, pl.ds(h * ROPE, ROPE)]
        g_ref[rows, :] = dot(go_ref[:, cols], vup_ref[:, cols], NT).astype(BF16)
    col, hi, core = where_ref[0], where_ref[1], where_ref[2]
    position = 2 * col + hi
    row = lax.broadcasted_iota(jnp.int32, bias_ref.shape, 0)
    query = lax.broadcasted_iota(jnp.int32, bias_ref.shape, 1)
    low = row & 15
    slot = (row >> 4) & 1
    source = (row >> 5) & 1
    lo = (row >> 6) & 3
    side = (row >> 8) ^ core
    back_even = jnp.where(slot == 0, 3 * source, 2 - source)
    back_odd = jnp.where(slot == 0, 1 - source, 3 - source)
    back = jnp.where(hi == 0, back_even, back_odd)
    token = (lo * 2 + side) * 16 + low
    kept = jnp.where(
        back == 1, keep_ref[0, 0], jnp.where(back == 2, keep_ref[0, 1], keep_ref[0, 2])
    )
    seen = jnp.where(
        back == 0,
        (token <= query).astype(jnp.int32),
        ((kept == 1) & (position >= back)).astype(jnp.int32),
    )
    bias_ref[...] = jnp.where(seen == 1, 0.0, -jnp.inf)


def stage_kernel(in_ref, out_ref):
    out_ref[...] = in_ref[...]


def pieces_kernel(latent_ref, back1_ref, back2_ref, out_ref):
    rows = latent_ref.shape[0]
    own, back1 = latent_ref[...], back1_ref[...]
    to_even = jnp.where(lax.axis_index("hi") == 1, back2_ref[...], own)
    for i in range(out_ref.shape[0]):
        out_ref[i, :rows] = to_even if i % 2 == 0 else own
        out_ref[i, rows:] = back1


def attend_kernel(mine_ref, mate_ref, ql_ref, g_ref, bias_ref, send_ref, ds_ref, wt_ref, lat_ref):
    half = mine_ref.shape[0]
    group = bias_ref.shape[1]
    pairs = ql_ref.shape[0] // (2 * group)
    lat_ref[:half] = mine_ref[...]
    lat_ref[half:] = mate_ref[...]
    for pair in range(pairs):
        cols = pl.ds(pair * 2 * group, 2 * group)
        bias = bias_ref[...]
        bias = jnp.concatenate([bias, bias], axis=1)
        scores = dot(lat_ref[...], ql_ref[cols, :], NT) * (SCALE * LOG2E) + bias
        top = jnp.max(scores, axis=0, keepdims=True)
        exponent = jnp.exp2(scores - top)
        probs = exponent * (1.0 / jnp.sum(exponent, axis=0, keepdims=True))
        weights = probs.astype(BF16)
        wt_ref[:, cols] = weights
        slopes = dot(lat_ref[:, :RANK], g_ref[cols, :], NT)
        delta = jnp.sum(weights.astype(F32) * slopes, axis=0, keepdims=True)
        ds_ref[:, cols] = (probs * ((slopes - delta) * SCALE)).astype(BF16)
    content = dot(ds_ref[half:, :], ql_ref[:, :RANK]) + dot(wt_ref[half:, :], g_ref[...])
    send_ref[:, :RANK] = content.astype(BF16)
    send_ref[:, RANK:] = dot(ds_ref[half:, :], ql_ref[:, RANK:]).astype(BF16)


def query_grads(heads, mine_ref, mate_ref, ds_ref, kup_ref, dqn_ref, dqr_ref):
    half = mine_ref.shape[0]
    group = dqn_ref.shape[0]
    for h in heads:
        cols = pl.ds(h * group, group)
        absorbed = dot(ds_ref[:half, cols], mine_ref[...], TN) + dot(ds_ref[half:, cols], mate_ref[...], TN)
        nope = pl.ds(h * NOPE, NOPE)
        dqn_ref[:, nope] = dot(absorbed[:, :RANK].astype(BF16), kup_ref[:, nope])
        dqr_ref[:, pl.ds(h * ROPE, ROPE)] = absorbed[:, RANK:]


def own_kernel(mine_ref, mate_ref, ds_ref, wt_ref, ql_ref, g_ref, kup_ref, own_ref, dqn_ref, dqr_ref):
    half = own_ref.shape[0]
    content = dot(ds_ref[:half, :], ql_ref[:, :RANK]) + dot(wt_ref[:half, :], g_ref[...])
    own_ref[:, :RANK] = content
    own_ref[:, RANK:] = dot(ds_ref[:half, :], ql_ref[:, RANK:])
    query_grads(range(EARLY), mine_ref, mate_ref, ds_ref, kup_ref, dqn_ref, dqr_ref)


def add_kernel(own_ref, arrived_ref, sum_ref):
    sum_ref[...] = (own_ref[...] + arrived_ref[...].astype(F32)).astype(BF16)


def query_kernel(mine_ref, mate_ref, ds_ref, kup_ref, early_n_ref, early_r_ref, dqn_ref, dqr_ref):
    dqn_ref[:, : EARLY * NOPE] = early_n_ref[...]
    dqr_ref[:, : EARLY * ROPE] = early_r_ref[...]
    heads = kup_ref.shape[1] // NOPE
    query_grads(range(EARLY, heads), mine_ref, mate_ref, ds_ref, kup_ref, dqn_ref, dqr_ref)


def owners_kernel(parts_ref, local_ref, to_back1_ref, to_back2_ref):
    rows = local_ref.shape[0]
    parts = [parts_ref[i].astype(F32) for i in range(parts_ref.shape[0])]
    even, odd = parts[0::2], parts[1::2]
    even, odd = sum(even[1:], even[0]), sum(odd[1:], odd[0])
    to_back1_ref[...] = (even[rows:] + odd[rows:]).astype(BF16)
    to_back2_ref[...] = even[:rows].astype(BF16)
    local_ref[...] = odd[:rows] + jnp.where(lax.axis_index("hi") == 0, even[:rows], 0.0)


def call(kernel, outs, specs, scratch=(), flops=0, nbytes=0):
    return pl.pallas_call(
        kernel,
        out_shape=[jax.ShapeDtypeStruct(s, t) for s, t in outs],
        in_specs=specs,
        out_specs=[VMEM] * len(outs),
        scratch_shapes=scratch,
        compiler_params=PARAMS,
        cost_estimate=pl.CostEstimate(flops=flops, bytes_accessed=nbytes, transcendentals=0),
    )


def on_device(query_nope, query_rope, grad_out, latent, key_up, value_up, block_keep):
    group = query_nope.shape[0]
    rows, width = latent.shape
    heads = key_up.shape[1] // NOPE
    columns = lax.axis_size("col")
    chips = lax.axis_size("hi") * lax.axis_size("lo")
    total = heads * group
    window = 4 * group
    half = window // 2
    where = jnp.stack([lax.axis_index(name) for name in ("col", "hi", "core")]).astype(jnp.int32)

    back1 = lax.ppermute(latent, "col", [(i, i + 1) for i in range(columns - 1)])
    back2 = lax.ppermute(latent, ("col", "hi"), [(2 * i + 1, 2 * i + 5) for i in range(columns - 2)])

    ql, g, bias = call(
        absorb_kernel,
        [((total, width), BF16), ((total, RANK), BF16), ((window, group), F32)],
        [SMEM, SMEM] + [VMEM] * 5,
        flops=4 * total * NOPE * RANK,
        nbytes=5 << 20,
    )(where, block_keep, query_nope, query_rope, grad_out, key_up, value_up)
    (staged,) = call(stage_kernel, [((rows, width), BF16)], [VMEM], flops=4 << 30, nbytes=4 << 20)(latent)
    (pieces,) = call(
        pieces_kernel,
        [((chips, 2 * rows, width), BF16)],
        [VMEM] * 3,
        flops=4 << 30,
        nbytes=4 << 20,
    )(staged, back1, back2)
    mine = lax.all_to_all(pieces, ("lo", "hi"), 0, 0, tiled=True).reshape(half, width)
    swap = [(0, 1), (1, 0)]
    mate = lax.ppermute(mine, "core", swap)
    send, ds, wt = call(
        attend_kernel,
        [((half, width), BF16), ((window, total), BF16), ((window, total), BF16)],
        [VMEM] * 5,
        scratch=[pltpu.VMEM((window, width), BF16)],
        flops=6 * total * window * width,
        nbytes=5 << 20,
    )(mine, mate, ql, g, bias)
    arrived = lax.ppermute(send, "core", swap)
    own, early_n, early_r = call(
        own_kernel,
        [((half, width), F32), ((group, EARLY * NOPE), F32), ((group, EARLY * ROPE), F32)],
        [VMEM] * 7,
        flops=4 * half * total * width,
        nbytes=4 << 20,
    )(mine, mate, ds, wt, ql, g, key_up)
    (summed,) = call(add_kernel, [((half, width), BF16)], [VMEM] * 2)(own, arrived)
    parts = lax.all_to_all(summed.reshape(chips, 2 * rows, width), ("lo", "hi"), 0, 0, tiled=True)
    local, to_back1, to_back2 = call(
        owners_kernel,
        [((rows, width), F32), ((rows, width), BF16), ((rows, width), BF16)],
        [VMEM],
    )(parts)
    d_nope, d_rope = call(
        query_kernel,
        [((group, heads * NOPE), F32), ((group, heads * ROPE), F32)],
        [VMEM] * 6,
        flops=2 * total * window * width + 2 * total * RANK * NOPE,
        nbytes=4 << 20,
    )(mine, mate, ds, key_up, early_n, early_r)
    came2 = lax.ppermute(to_back2, ("col", "hi"), [(2 * i + 5, 2 * i + 1) for i in range(columns - 2)])
    came1 = lax.ppermute(to_back1, "col", [(i + 1, i) for i in range(columns - 1)])
    d_latent = local + came1.astype(F32) + came2.astype(F32)
    return (d_nope, d_rope, d_latent)


def solution(mesh):
    fine = Mesh(mesh.devices.reshape(-1, 2, 4, 2), ("col", "hi", "lo", "core"))
    ctx, head = ("col", "hi"), ("lo", "core")
    placed = (
        P(ctx, head),
        P(ctx, head),
        P(ctx, head),
        P((*ctx, *head), None),
        P(None, head),
        P(None, head),
        P(ctx, None),
    )
    return jax.shard_map(
        on_device,
        mesh=fine,
        in_specs=placed,
        out_specs=(P(ctx, head), P(ctx, head), P((*ctx, *head), None)),
        check_vma=False,
    )
```

```python
import math

import jax
import jax.numpy as jnp
import numpy as np
from jax import lax
from jax.experimental import pallas as pl
from jax.experimental.pallas import tpu as pltpu
from jax.sharding import Mesh, PartitionSpec as P

NOPE = 128
ROPE = 64
VDIM = 128
RANK = 512
WIDTH = RANK + ROPE
SCALE = 1.0 / math.sqrt(NOPE + ROPE)
LOG2E = 1.4426950408889634
EARLY = 2
PEERS = [[0, 4, 2, 6, 1, 5, 3, 7]]
BF16 = jnp.bfloat16
F32 = jnp.float32
NT = (((1,), (1,)), ((), ()))
TN = (((0,), (0,)), ((), ()))
VMEM = pl.BlockSpec(memory_space=pltpu.VMEM)
SMEM = pl.BlockSpec(memory_space=pltpu.SMEM)
PARAMS = pltpu.CompilerParams(vmem_limit_bytes=16 * 1024 * 1024)


def dot(a, b, dims=(((1,), (0,)), ((), ()))):
    return lax.dot_general(a, b, dims, preferred_element_type=F32)


def absorb_kernel(where_ref, keep_ref, qn_ref, qr_ref, go_ref, kup_ref, vup_ref, ql_ref, g_ref, bias_ref):
    heads = kup_ref.shape[1] // NOPE
    group = qn_ref.shape[0]
    for h in range(heads):
        rows = pl.ds(h * group, group)
        cols = pl.ds(h * NOPE, NOPE)
        ql_ref[rows, :RANK] = dot(qn_ref[:, cols], kup_ref[:, cols], NT).astype(BF16)
        ql_ref[rows, RANK:] = qr_ref[:, pl.ds(h * ROPE, ROPE)]
        g_ref[rows, :] = dot(go_ref[:, cols], vup_ref[:, cols], NT).astype(BF16)
    col, hi, core = where_ref[0], where_ref[1], where_ref[2]
    position = 2 * col + hi
    row = lax.broadcasted_iota(jnp.int32, bias_ref.shape, 0)
    query = lax.broadcasted_iota(jnp.int32, bias_ref.shape, 1)
    low = row & 15
    slot = (row >> 4) & 1
    source = (row >> 5) & 1
    lo = ((row >> 7) & 1) | ((row >> 5) & 2)
    side = (row >> 8) ^ core
    back_even = jnp.where(slot == 0, 3 * source, 2 - source)
    back_odd = jnp.where(slot == 0, 1 - source, 3 - source)
    back = jnp.where(hi == 0, back_even, back_odd)
    token = (lo * 2 + side) * 16 + low
    kept = jnp.where(
        back == 1, keep_ref[0, 0], jnp.where(back == 2, keep_ref[0, 1], keep_ref[0, 2])
    )
    seen = jnp.where(
        back == 0,
        (token <= query).astype(jnp.int32),
        ((kept == 1) & (position >= back)).astype(jnp.int32),
    )
    bias_ref[...] = jnp.where(seen == 1, 0.0, -jnp.inf)


def stage_kernel(in_ref, out_ref):
    out_ref[...] = in_ref[...]


def pieces_kernel(latent_ref, back1_ref, back2_ref, out_ref):
    rows = latent_ref.shape[0]
    own, back1 = latent_ref[...], back1_ref[...]
    to_even = jnp.where(lax.axis_index("hi") == 1, back2_ref[...], own)
    for i in range(out_ref.shape[0]):
        out_ref[i, :rows] = to_even if i % 2 == 0 else own
        out_ref[i, rows:] = back1


def attend_kernel(mine_ref, mate_ref, ql_ref, g_ref, bias_ref, send_ref, ds_ref, wt_ref, lat_ref):
    half = mine_ref.shape[0]
    group = bias_ref.shape[1]
    pairs = ql_ref.shape[0] // (2 * group)
    lat_ref[:half] = mine_ref[...]
    lat_ref[half:] = mate_ref[...]
    for pair in range(pairs):
        cols = pl.ds(pair * 2 * group, 2 * group)
        bias = bias_ref[...]
        bias = jnp.concatenate([bias, bias], axis=1)
        scores = dot(lat_ref[...], ql_ref[cols, :], NT) * (SCALE * LOG2E) + bias
        top = jnp.max(scores, axis=0, keepdims=True)
        exponent = jnp.exp2(scores - top)
        probs = exponent * (1.0 / jnp.sum(exponent, axis=0, keepdims=True))
        weights = probs.astype(BF16)
        wt_ref[:, cols] = weights
        slopes = dot(lat_ref[:, :RANK], g_ref[cols, :], NT)
        delta = jnp.sum(weights.astype(F32) * slopes, axis=0, keepdims=True)
        ds_ref[:, cols] = (probs * ((slopes - delta) * SCALE)).astype(BF16)
    content = dot(ds_ref[half:, :], ql_ref[:, :RANK]) + dot(wt_ref[half:, :], g_ref[...])
    send_ref[:, :RANK] = content.astype(BF16)
    send_ref[:, RANK:] = dot(ds_ref[half:, :], ql_ref[:, RANK:]).astype(BF16)


def query_grads(heads, mine_ref, mate_ref, ds_ref, kup_ref, dqn_ref, dqr_ref):
    half = mine_ref.shape[0]
    group = dqn_ref.shape[0]
    for h in heads:
        cols = pl.ds(h * group, group)
        absorbed = dot(ds_ref[:half, cols], mine_ref[...], TN) + dot(ds_ref[half:, cols], mate_ref[...], TN)
        nope = pl.ds(h * NOPE, NOPE)
        dqn_ref[:, nope] = dot(absorbed[:, :RANK].astype(BF16), kup_ref[:, nope])
        dqr_ref[:, pl.ds(h * ROPE, ROPE)] = absorbed[:, RANK:]


def own_kernel(mine_ref, mate_ref, ds_ref, wt_ref, ql_ref, g_ref, kup_ref, own_ref, dqn_ref, dqr_ref):
    half = own_ref.shape[0]
    content = dot(ds_ref[:half, :], ql_ref[:, :RANK]) + dot(wt_ref[:half, :], g_ref[...])
    own_ref[:, :RANK] = content
    own_ref[:, RANK:] = dot(ds_ref[:half, :], ql_ref[:, RANK:])
    query_grads(range(EARLY), mine_ref, mate_ref, ds_ref, kup_ref, dqn_ref, dqr_ref)


def add_kernel(own_ref, arrived_ref, sum_ref):
    sum_ref[...] = (own_ref[...] + arrived_ref[...].astype(F32)).astype(BF16)


def query_kernel(mine_ref, mate_ref, ds_ref, kup_ref, early_n_ref, early_r_ref, dqn_ref, dqr_ref):
    dqn_ref[:, : EARLY * NOPE] = early_n_ref[...]
    dqr_ref[:, : EARLY * ROPE] = early_r_ref[...]
    heads = kup_ref.shape[1] // NOPE
    query_grads(range(EARLY, heads), mine_ref, mate_ref, ds_ref, kup_ref, dqn_ref, dqr_ref)


def owners_kernel(parts_ref, local_ref, to_back1_ref, to_back2_ref):
    rows = local_ref.shape[0]
    parts = [parts_ref[i].astype(F32) for i in range(parts_ref.shape[0])]
    even, odd = parts[0::2], parts[1::2]
    even, odd = sum(even[1:], even[0]), sum(odd[1:], odd[0])
    to_back1_ref[...] = (even[rows:] + odd[rows:]).astype(BF16)
    to_back2_ref[...] = even[:rows].astype(BF16)
    local_ref[...] = odd[:rows] + jnp.where(lax.axis_index("hi") == 0, even[:rows], 0.0)


def call(kernel, outs, specs, scratch=(), flops=0, nbytes=0):
    return pl.pallas_call(
        kernel,
        out_shape=[jax.ShapeDtypeStruct(s, t) for s, t in outs],
        in_specs=specs,
        out_specs=[VMEM] * len(outs),
        scratch_shapes=scratch,
        compiler_params=PARAMS,
        cost_estimate=pl.CostEstimate(flops=flops, bytes_accessed=nbytes, transcendentals=0),
    )


def on_device(query_nope, query_rope, grad_out, latent, key_up, value_up, block_keep):
    group = query_nope.shape[0]
    rows, width = latent.shape
    heads = key_up.shape[1] // NOPE
    columns = lax.axis_size("col")
    chips = lax.axis_size("hi") * lax.axis_size("lo")
    total = heads * group
    window = 4 * group
    half = window // 2
    where = jnp.stack([lax.axis_index(name) for name in ("col", "hi", "core")]).astype(jnp.int32)

    back1 = lax.ppermute(latent, "col", [(i, i + 1) for i in range(columns - 1)])
    back2 = lax.ppermute(latent, ("col", "hi"), [(2 * i + 1, 2 * i + 5) for i in range(columns - 2)])

    ql, g, bias = call(
        absorb_kernel,
        [((total, width), BF16), ((total, RANK), BF16), ((window, group), F32)],
        [SMEM, SMEM] + [VMEM] * 5,
        flops=4 * total * NOPE * RANK,
        nbytes=5 << 20,
    )(where, block_keep, query_nope, query_rope, grad_out, key_up, value_up)
    (staged,) = call(stage_kernel, [((rows, width), BF16)], [VMEM], flops=4 << 30, nbytes=4 << 20)(latent)
    (pieces,) = call(
        pieces_kernel,
        [((chips, 2 * rows, width), BF16)],
        [VMEM] * 3,
        flops=4 << 30,
        nbytes=4 << 20,
    )(staged, back1, back2)
    mine = lax.all_to_all(pieces, ("hi", "lo"), 0, 0, axis_index_groups=PEERS, tiled=True).reshape(half, width)
    swap = [(0, 1), (1, 0)]
    mate = lax.ppermute(mine, "core", swap)
    send, ds, wt = call(
        attend_kernel,
        [((half, width), BF16), ((window, total), BF16), ((window, total), BF16)],
        [VMEM] * 5,
        scratch=[pltpu.VMEM((window, width), BF16)],
        flops=6 * total * window * width,
        nbytes=5 << 20,
    )(mine, mate, ql, g, bias)
    arrived = lax.ppermute(send, "core", swap)
    own, early_n, early_r = call(
        own_kernel,
        [((half, width), F32), ((group, EARLY * NOPE), F32), ((group, EARLY * ROPE), F32)],
        [VMEM] * 7,
        flops=4 * half * total * width,
        nbytes=4 << 20,
    )(mine, mate, ds, wt, ql, g, key_up)
    (summed,) = call(add_kernel, [((half, width), BF16)], [VMEM] * 2)(own, arrived)
    parts = lax.all_to_all(summed.reshape(chips, 2 * rows, width), ("hi", "lo"), 0, 0, axis_index_groups=PEERS, tiled=True)
    local, to_back1, to_back2 = call(
        owners_kernel,
        [((rows, width), F32), ((rows, width), BF16), ((rows, width), BF16)],
        [VMEM],
    )(parts)
    d_nope, d_rope = call(
        query_kernel,
        [((group, heads * NOPE), F32), ((group, heads * ROPE), F32)],
        [VMEM] * 6,
        flops=2 * total * window * width + 2 * total * RANK * NOPE,
        nbytes=4 << 20,
    )(mine, mate, ds, key_up, early_n, early_r)
    came2 = lax.ppermute(to_back2, ("col", "hi"), [(2 * i + 5, 2 * i + 1) for i in range(columns - 2)])
    came1 = lax.ppermute(to_back1, "col", [(i + 1, i) for i in range(columns - 1)])
    d_latent = local + came1.astype(F32) + came2.astype(F32)
    return (d_nope, d_rope, d_latent)


def solution(mesh):
    fine = Mesh(mesh.devices.reshape(-1, 2, 4, 2), ("col", "hi", "lo", "core"))
    ctx, head = ("col", "hi"), ("lo", "core")
    placed = (
        P(ctx, head),
        P(ctx, head),
        P(ctx, head),
        P((*ctx, *head), None),
        P(None, head),
        P(None, head),
        P(ctx, None),
    )
    return jax.shard_map(
        on_device,
        mesh=fine,
        in_specs=placed,
        out_specs=(P(ctx, head), P(ctx, head), P((*ctx, *head), None)),
        check_vma=False,
    )
```
